32 devices in a mesh: tv: 8 (over z, core), sv: 4 (over y, x).
Axes of the slice: x: 2, y: 2, z: 4, core: 2. Of those that a mesh axis runs over, the one named last changes fastest.
Arguments:
- teacher_hidden: bfloat16 [512, 4096], P('tv', 'sv'), may hold values from -250 to 250
- student_hidden: bfloat16 [512, 5120], P('sv', 'tv'), may hold values from -250 to 250
- teacher_head: bfloat16 [4096, 151936], P('sv', 'tv'), may hold values from -0.09375 to 0.09375
- student_head: bfloat16 [5120, 151936], P('tv', 'sv'), may hold values from -0.078125 to 0.078125
- token_ids: int32 [512], P('tv'), may hold values from 0 to 151935
Outputs:
- rewards: float32 [512], P('tv')
- kl_div: float32 [512], P('tv')
- logit_grad: bfloat16 [512, 151936], P('tv', 'sv')
The draws below stay inside these ranges and needn't reach their ends.
All inputs are finite; a program needn't handle non-finite values.
Results may differ from the reference program's by a relative error of at most 0.0042.
Values may be sent and summed in bfloat16 or wider, within the bound.
A program may use at most 320 MiB of HBM per device.

```python
import math
import jax
import jax.numpy as jnp
import numpy as np

DT = 4096
DS = 5120
V = 151936
TOKENS = 512


def scaled_rows(key, row_total, col_total, low, high, spike):
    key_values, key_scales, key_phase = jax.random.split(key, 3)
    values = jnp.clip(jax.random.normal(key_values, (row_total, col_total), jnp.float32), -4.0, 4.0)
    scales = jnp.exp(jax.random.uniform(key_scales, (row_total, 1), jnp.float32, math.log(low), math.log(high)))
    phase = jax.random.randint(key_phase, (), 0, 29)
    row_index = jnp.arange(row_total)[:, None]
    scales = jnp.where(row_index % 29 == phase, spike, scales)
    return (values * scales).astype(jnp.bfloat16)


def draw_teacher_hidden(key, part):
    key = jax.random.fold_in(key, 11)
    return scaled_rows(key, TOKENS, DT, 0.3, 3.0, 1.0)


def draw_student_hidden(key, part):
    key = jax.random.fold_in(key, 23)
    return scaled_rows(key, TOKENS, DS, 0.3, 3.0, 1.0)


def touch_ends(drawn, rng, smallest, high):
    index_at = [jax.random.randint(jax.random.fold_in(rng, axis), (), 0, length) for axis, length in enumerate(drawn.shape)]
    widest = drawn.shape.index(max(drawn.shape))
    neighbour = index_at[:widest] + [(index_at[widest] + 1) % drawn.shape[widest]] + index_at[widest + 1:]
    return drawn.at[tuple(index_at)].set(smallest).at[tuple(neighbour)].set(high)


def level_of(key, dims, shards, low, top_value):
    factor_of = 1.0
    for position, blocks in shards:
        heights = jax.random.uniform(jax.random.fold_in(jax.random.fold_in(key, 6), position), (blocks,), jnp.float32, low / len(shards), top_value / len(shards))
        factor_of = factor_of * jnp.repeat(jnp.exp(heights), dims[position] // blocks).reshape((-1,) + (1,) * (len(dims) - 1 - position))
    return factor_of


def skewed_wide(stream_key, dims, amount, lean):
    loads = [min(1 << octave, amount + 1 - (1 << octave)) * (1 << 20) // math.isqrt((1 << octave) ** lean) + 1 for octave in range((amount + 1).bit_length()) if 1 << octave <= amount]
    scale = 1 + sum(loads) // (1 << 30)
    grid = np.cumsum(np.array([max(1, weight // scale) for weight in loads]))
    lot = jax.random.randint(jax.random.fold_in(stream_key, 1), dims, 0, int(grid[len(loads) - 1]))
    start = jnp.left_shift(1, jnp.searchsorted(jnp.asarray(grid, jnp.int32), lot, side="right").astype(jnp.int32))
    rank = start - 1 + jax.random.randint(jax.random.fold_in(stream_key, 4), dims, 0, 1 << 30) % jnp.minimum(start, amount + 1 - start)
    return jax.random.permutation(jax.random.fold_in(stream_key, 2), amount)[rank].astype(jnp.int32)


def gaussian(rng, shape, deviation, most, cuts=(), kind=jnp.bfloat16):
    result = jax.random.normal(rng, shape, jnp.float32) * deviation
    if len(cuts) > 0:
        result = level_of(rng, shape, cuts, -0.22, 0.18) * result
    return jnp.clip(result, min=-most, max=most).astype(kind)


def setup_inputs(seed: int = 0) -> dict:
    seeds = jax.random.split(jax.random.key(seed), 6)
    teacher_hidden = draw_teacher_hidden(jax.random.fold_in(seeds[5], 71), 0)
    student_hidden = draw_student_hidden(jax.random.fold_in(seeds[5], 71), 0)
    teacher_head = gaussian(seeds[2], (DT, V), DT ** -0.5, 0.09375, ((0, 4), (1, 8)))
    student_head = gaussian(seeds[3], (DS, V), DS ** -0.5, 0.078125, ((0, 8), (1, 4)))
    token_ids = touch_ends(skewed_wide(seeds[4], (TOKENS,), V, 2), jax.random.fold_in(seeds[4], 3), 0, V - 1).astype(jnp.int32)
    return {"teacher_hidden": teacher_hidden, "student_hidden": student_hidden, "teacher_head": teacher_head, "student_head": student_head, "token_ids": token_ids}


def reference(teacher_hidden, student_hidden, teacher_head, student_head, token_ids):
    teacher_logits = jnp.dot(teacher_hidden, teacher_head, preferred_element_type=jnp.float32).astype(jnp.bfloat16)
    student_logits = jnp.dot(student_hidden, student_head, preferred_element_type=jnp.float32)
    teacher_wide = teacher_logits.astype(jnp.float32)
    teacher_logprob = teacher_wide - jax.nn.logsumexp(teacher_wide, axis=1, keepdims=True)
    student_logprob = student_logits - jax.nn.logsumexp(student_logits, axis=1, keepdims=True)
    student_prob = jnp.exp(student_logprob)
    log_ratio = student_logprob - teacher_logprob
    kl_div = jnp.sum(student_prob * log_ratio, axis=1)
    picked = jnp.take_along_axis(-log_ratio, token_ids[:, None], axis=1)[:, 0]
    logit_grad = (student_prob * (log_ratio - kl_div[:, None])).astype(jnp.bfloat16)
    return picked, kl_div, logit_grad
```

```python
import jax
import jax.numpy as jnp
from jax import lax
from jax.sharding import PartitionSpec as P

CHUNKS = 4
WIRE = jnp.float16
SHRINK = 0.25
STEPS = 64.0
TOP = 32000.0


def cut_words(width):
    step = max(128, width // CHUNKS // 128 * 128)
    edges = [step * k for k in range(CHUNKS)] + [width]
    return [(low, high) for low, high in zip(edges[:-1], edges[1:]) if high > low]


def pack(values):
    return (values * SHRINK).astype(WIRE)


def unpack(values):
    return values.astype(jnp.float32) * (1.0 / SHRINK)


def quantize(values, limit):
    code = jnp.ceil(jnp.log2(jnp.maximum(limit, 1e-20)) * STEPS + 0.5)
    scaled = values * (TOP * jnp.exp2(code * (-1.0 / STEPS)))
    tail = jnp.broadcast_to(code, (values.shape[0], 128))
    return jnp.concatenate([scaled, tail], axis=1).round().astype(jnp.int16)


def restore(coded):
    limit = jnp.exp2(coded[:, -1:].astype(jnp.float32) * (1.0 / STEPS))
    return coded[:, :-128].astype(jnp.float32) * (limit * (1.0 / TOP)), limit


def block(array, index):
    return lax.dynamic_index_in_dim(array, index, 0, keepdims=False)


def reduce_teacher(teacher_hidden, teacher_head):
    tv_count, sv_count = lax.axis_size("tv"), lax.axis_size("sv")
    here = lax.axis_index("sv")
    rows = lax.all_gather(teacher_hidden, "tv", axis=0, tiled=True)
    share = rows.shape[0] // (tv_count * sv_count)
    rows = rows.reshape(tv_count, sv_count, share, rows.shape[1])
    rows = rows.transpose(1, 0, 2, 3).reshape(-1, rows.shape[-1])
    part = pack(jnp.dot(rows, teacher_head, preferred_element_type=jnp.float32))
    part = part.reshape(sv_count, tv_count * share, part.shape[1])
    total = unpack(block(part, here))
    for flip in range(1, sv_count):
        swap = [(i, i ^ flip) for i in range(sv_count)]
        total = total + unpack(lax.ppermute(block(part, here ^ flip), "sv", swap))
    return total.astype(jnp.bfloat16).reshape(tv_count, share, part.shape[2])


def place_teacher(logit):
    tv_count, sv_count = lax.axis_size("tv"), lax.axis_size("sv")
    outer = tv_count // 2
    tv, sv = lax.axis_index("tv"), lax.axis_index("sv")
    plane, core = tv // 2, tv % 2
    got = []
    for flip in range(2):
        row = []
        for k in range(sv_count):
            pairs = []
            for z in range(outer):
                for c in range(2):
                    for s in range(sv_count):
                        to_tv = (s + k) % outer * 2 + (c ^ flip)
                        pairs.append(((z * 2 + c) * sv_count + s, to_tv * sv_count + z))
            mine = block(logit, (sv + k) % outer * 2 + (core ^ flip))
            row.append(lax.ppermute(mine, ("tv", "sv"), pairs))
        got.append(jnp.stack(row))
    first = jnp.where(core == 0, got[0], got[1])
    second = jnp.where(core == 0, got[1], got[0])
    halves = []
    for half in (first, second):
        groups = [block(half, (plane - g) % outer) for g in range(sv_count)]
        halves.append(jnp.concatenate(groups, axis=0))
    return jnp.concatenate(halves, axis=1)


def reduce_student(rows, head):
    tv_count = lax.axis_size("tv")
    outer = tv_count // 2
    plane = lax.axis_index("tv") // 2
    given = pack(jnp.dot(rows[1], head, preferred_element_type=jnp.float32))
    kept = jnp.dot(rows[0], head, preferred_element_type=jnp.float32)
    across = lax.ppermute(given, "tv", [(i, i ^ 1) for i in range(tv_count)])
    chip = (kept + unpack(across)).reshape(outer, -1, head.shape[1])
    peak = jnp.max(jnp.abs(chip), axis=2, keepdims=True)
    up = down = None
    for step in range(outer - 1):
        above = jnp.minimum(plane + outer - 1 - step, outer - 1)
        below = jnp.maximum(plane - (outer - 1 - step), 0)
        send_up, limit_up = block(chip, above), block(peak, above)
        send_down, limit_down = block(chip, below), block(peak, below)
        if step:
            (more_up, extra_up), (more_down, extra_down) = restore(up), restore(down)
            send_up, limit_up = send_up + more_up, limit_up + extra_up
            send_down, limit_down = send_down + more_down, limit_down + extra_down
        up_pairs = [(2 * z + c, 2 * z + 2 + c) for z in range(min(step + 1, outer - 1)) for c in range(2)]
        down_pairs = [(tv_count - 1 - a, tv_count - 1 - b) for a, b in up_pairs]
        up = lax.ppermute(quantize(send_up, limit_up), "tv", up_pairs)
        down = lax.ppermute(quantize(send_down, limit_down), "tv", down_pairs)
    return block(chip, plane) + restore(up)[0] + restore(down)[0]


def masses(student, teacher, low, token_ids):
    gap = student - teacher
    words = low + lax.broadcasted_iota(jnp.int32, student.shape, 1)
    picked = jnp.sum(jnp.where(words == token_ids[:, None], -gap, 0.0), axis=1)
    peak_s = jnp.max(student, axis=1)
    weight = jnp.exp(student - peak_s[:, None])
    peak_t = jnp.max(teacher, axis=1)
    mass_t = jnp.sum(jnp.exp(teacher - peak_t[:, None]), axis=1)
    return jnp.stack(
        [peak_s, jnp.sum(weight, axis=1), jnp.sum(weight * gap, axis=1), peak_t, mass_t, picked]
    )


def shards(teacher_hidden, student_hidden, teacher_head, student_head, token_ids):
    tv_count = lax.axis_size("tv")
    core = lax.axis_index("tv") % 2
    teacher_logit = reduce_teacher(teacher_hidden, teacher_head)
    rows = lax.all_gather(student_hidden, "sv", axis=0, tiled=True)
    rows = rows.reshape(tv_count // 2, 2, -1, rows.shape[1]).transpose(1, 0, 2, 3)
    rows = rows.reshape(2, -1, rows.shape[3])
    rows = jnp.stack([block(rows, core), block(rows, 1 - core)])
    cuts = cut_words(student_head.shape[1])
    student = [reduce_student(rows, student_head[:, low:high]) for low, high in cuts]
    teacher = place_teacher(teacher_logit)
    teacher = [teacher[:, low:high].astype(jnp.float32) for low, high in cuts]
    start = lax.axis_index("sv") * student_head.shape[1]
    local = jnp.stack(
        [masses(s, t, start + low, token_ids) for s, t, (low, _) in zip(student, teacher, cuts)]
    )
    stats = lax.all_gather(local, "sv", axis=0, tiled=True)
    peak_s, mass_s, gap_s, peak_t, mass_t, picked = [stats[:, k] for k in range(6)]
    top_s, top_t = jnp.max(peak_s, axis=0), jnp.max(peak_t, axis=0)
    scale_s = jnp.exp(peak_s - top_s)
    sum_s = jnp.sum(mass_s * scale_s, axis=0)
    sum_t = jnp.sum(mass_t * jnp.exp(peak_t - top_t), axis=0)
    norm_s, norm_t = top_s + jnp.log(sum_s), top_t + jnp.log(sum_t)
    mean_gap = jnp.sum(gap_s * scale_s, axis=0) / sum_s
    kl_div = mean_gap - norm_s + norm_t
    rewards = jnp.sum(picked, axis=0) + norm_s - norm_t
    grad = [
        (jnp.exp(s - norm_s[:, None]) * (s - t - mean_gap[:, None])).astype(jnp.bfloat16)
        for s, t in zip(student, teacher)
    ]
    return (rewards, kl_div, jnp.concatenate(grad, axis=1))


def solution(mesh):
    in_specs = (P("tv", "sv"), P("sv", "tv"), P("sv", "tv"), P("tv", "sv"), P("tv"))
    out_specs = (P("tv"), P("tv"), P("tv", "sv"))
    return jax.shard_map(shards, mesh=mesh, in_specs=in_specs, out_specs=out_specs, check_vma=False)
```

```python
import jax
import jax.numpy as jnp
from jax import lax
from jax.sharding import PartitionSpec as P

CHUNKS = 4
WIRE = jnp.float16
SHRINK = 0.25
STEPS = 64.0
TOP = 32000.0


def cut_words(width):
    step = max(128, width // CHUNKS // 128 * 128)
    edges = [step * k for k in range(CHUNKS)] + [width]
    return [(low, high) for low, high in zip(edges[:-1], edges[1:]) if high > low]


def pack(values):
    return (values * SHRINK).astype(WIRE)


def unpack(values):
    return values.astype(jnp.float32) * (1.0 / SHRINK)


def quantize(values, limit):
    code = jnp.ceil(jnp.log2(jnp.maximum(limit, 1e-20)) * STEPS + 0.5)
    scaled = values * (TOP * jnp.exp2(code * (-1.0 / STEPS)))
    tail = jnp.broadcast_to(code, (values.shape[0], 128))
    return jnp.concatenate([scaled, tail], axis=1).round().astype(jnp.int16)


def restore(coded):
    limit = jnp.exp2(coded[:, -1:].astype(jnp.float32) * (1.0 / STEPS))
    return coded[:, :-128].astype(jnp.float32) * (limit * (1.0 / TOP)), limit


def block(array, index):
    return lax.dynamic_index_in_dim(array, index, 0, keepdims=False)


def reduce_teacher(teacher_hidden, teacher_head):
    tv_count, sv_count = lax.axis_size("tv"), lax.axis_size("sv")
    here = lax.axis_index("sv")
    rows = lax.all_gather(teacher_hidden, "tv", axis=0, tiled=True)
    share = rows.shape[0] // (tv_count * sv_count)
    rows = rows.reshape(tv_count, sv_count, share, rows.shape[1])
    rows = rows.transpose(1, 0, 2, 3).reshape(-1, rows.shape[-1])
    part = pack(jnp.dot(rows, teacher_head, preferred_element_type=jnp.float32))
    depth = tv_count * share
    total = unpack(lax.dynamic_slice_in_dim(part, here * depth, depth))
    for flip in range(1, sv_count):
        swap = [(i, i ^ flip) for i in range(sv_count)]
        given = lax.dynamic_slice_in_dim(part, (here ^ flip) * depth, depth)
        total = total + unpack(lax.ppermute(given, "sv", swap))
    return total.astype(jnp.bfloat16).reshape(tv_count, share, part.shape[1])


def place_teacher(logit):
    tv_count, sv_count = lax.axis_size("tv"), lax.axis_size("sv")
    outer = tv_count // 2
    tv, sv = lax.axis_index("tv"), lax.axis_index("sv")
    plane, core = tv // 2, tv % 2
    got = []
    for flip in range(2):
        row = []
        for k in range(sv_count):
            pairs = []
            for z in range(outer):
                for c in range(2):
                    for s in range(sv_count):
                        to_tv = (s + k) % outer * 2 + (c ^ flip)
                        pairs.append(((z * 2 + c) * sv_count + s, to_tv * sv_count + z))
            mine = block(logit, (sv + k) % outer * 2 + (core ^ flip))
            row.append(lax.ppermute(mine, ("tv", "sv"), pairs))
        got.append(jnp.stack(row))
    first = jnp.where(core == 0, got[0], got[1])
    second = jnp.where(core == 0, got[1], got[0])
    halves = []
    for half in (first, second):
        groups = [block(half, (plane - g) % outer) for g in range(sv_count)]
        halves.append(jnp.concatenate(groups, axis=0))
    return jnp.concatenate(halves, axis=1)


def reduce_student(rows, head):
    tv_count = lax.axis_size("tv")
    outer = tv_count // 2
    plane = lax.axis_index("tv") // 2
    given = pack(jnp.dot(rows[1], head, preferred_element_type=jnp.float32))
    kept = jnp.dot(rows[0], head, preferred_element_type=jnp.float32)
    across = lax.ppermute(given, "tv", [(i, i ^ 1) for i in range(tv_count)])
    chip = (kept + unpack(across)).reshape(outer, -1, head.shape[1])
    peak = jnp.max(jnp.abs(chip), axis=2, keepdims=True)
    up = down = None
    for step in range(outer - 1):
        above = jnp.minimum(plane + outer - 1 - step, outer - 1)
        below = jnp.maximum(plane - (outer - 1 - step), 0)
        send_up, limit_up = block(chip, above), block(peak, above)
        send_down, limit_down = block(chip, below), block(peak, below)
        if step:
            (more_up, extra_up), (more_down, extra_down) = restore(up), restore(down)
            send_up, limit_up = send_up + more_up, limit_up + extra_up
            send_down, limit_down = send_down + more_down, limit_down + extra_down
        up_pairs = [(2 * z + c, 2 * z + 2 + c) for z in range(min(step + 1, outer - 1)) for c in range(2)]
        down_pairs = [(tv_count - 1 - a, tv_count - 1 - b) for a, b in up_pairs]
        up = lax.ppermute(quantize(send_up, limit_up), "tv", up_pairs)
        down = lax.ppermute(quantize(send_down, limit_down), "tv", down_pairs)
    return block(chip, plane) + restore(up)[0] + restore(down)[0]


def masses(student, teacher, low, token_ids):
    gap = student - teacher
    words = low + lax.broadcasted_iota(jnp.int32, student.shape, 1)
    picked = jnp.sum(jnp.where(words == token_ids[:, None], -gap, 0.0), axis=1)
    peak_s = jnp.max(student, axis=1)
    weight = jnp.exp(student - peak_s[:, None])
    peak_t = jnp.max(teacher, axis=1)
    mass_t = jnp.sum(jnp.exp(teacher - peak_t[:, None]), axis=1)
    return jnp.stack(
        [peak_s, jnp.sum(weight, axis=1), jnp.sum(weight * gap, axis=1), peak_t, mass_t, picked]
    )


def shards(teacher_hidden, student_hidden, teacher_head, student_head, token_ids):
    tv_count = lax.axis_size("tv")
    core = lax.axis_index("tv") % 2
    teacher_logit = reduce_teacher(teacher_hidden, teacher_head)
    rows = lax.all_gather(student_hidden, "sv", axis=0, tiled=True)
    rows = rows.reshape(tv_count // 2, 2, -1, rows.shape[1]).transpose(1, 0, 2, 3)
    rows = rows.reshape(2, -1, rows.shape[3])
    rows = jnp.stack([block(rows, core), block(rows, 1 - core)])
    cuts = cut_words(student_head.shape[1])
    student = [reduce_student(rows, student_head[:, low:high]) for low, high in cuts]
    teacher = place_teacher(teacher_logit)
    teacher = [teacher[:, low:high].astype(jnp.float32) for low, high in cuts]
    start = lax.axis_index("sv") * student_head.shape[1]
    local = jnp.stack(
        [masses(s, t, start + low, token_ids) for s, t, (low, _) in zip(student, teacher, cuts)]
    )
    stats = lax.all_gather(local, "sv", axis=0, tiled=True)
    peak_s, mass_s, gap_s, peak_t, mass_t, picked = [stats[:, k] for k in range(6)]
    top_s, top_t = jnp.max(peak_s, axis=0), jnp.max(peak_t, axis=0)
    scale_s = jnp.exp(peak_s - top_s)
    sum_s = jnp.sum(mass_s * scale_s, axis=0)
    sum_t = jnp.sum(mass_t * jnp.exp(peak_t - top_t), axis=0)
    norm_s, norm_t = top_s + jnp.log(sum_s), top_t + jnp.log(sum_t)
    mean_gap = jnp.sum(gap_s * scale_s, axis=0) / sum_s
    kl_div = mean_gap - norm_s + norm_t
    rewards = jnp.sum(picked, axis=0) + norm_s - norm_t
    grad = [
        (jnp.exp(s - norm_s[:, None]) * (s - t - mean_gap[:, None])).astype(jnp.bfloat16)
        for s, t in zip(student, teacher)
    ]
    return (rewards, kl_div, jnp.concatenate(grad, axis=1))


def solution(mesh):
    in_specs = (P("tv", "sv"), P("sv", "tv"), P("sv", "tv"), P("tv", "sv"), P("tv"))
    out_specs = (P("tv"), P("tv"), P("tv", "sv"))
    return jax.shard_map(shards, mesh=mesh, in_specs=in_specs, out_specs=out_specs, check_vma=False)
```
